128 devices in a mesh: section: 16 (over x, y_lo, core), rep: 8 (over y_hi, z).
Axes of the slice: x: 4, y: 4 (y_hi: 2, y_lo: 2; y = y_hi * 2 + y_lo), z: 4, core: 2. Of those that a mesh axis runs over, the one named last changes fastest.
Arguments:
- patches: bfloat16 [8, 64, 256, 1792], P('rep', 'section'), may hold values from -30 to 30
- counts: int32 [8, 16], P('rep', 'section'), may hold values from 0 to 4, as said below
- gain: float32 [1792], replicated, may hold values from 0.5 to 1.5
- w_qkv: bfloat16 [1792, 2688], replicated, may hold values from -9 to 9
- cotangent: bfloat16 [8, 64, 256, 896], P('rep', 'section'), may hold values from -0.0625 to 0.0625
Outputs:
- encoded: bfloat16 [8, 64, 256, 896], P('rep', 'section')
- gradient_query_key_value: float32 [1792, 2688], P('section', 'rep')
- grad_gain: float32 [1792], replicated
The draws below stay inside these ranges and needn't reach their ends.
Inputs may be any that keep to these rules, and one draw needn't show every extreme that they name: `counts`: every replica has a device holding exactly 4 images.
All inputs are finite; a program needn't handle non-finite values.
Results may differ from the reference program's by a relative error of at most 0.024.
Values may be sent and summed in bfloat16 or wider, within the bound.
No kernel may reach another device: no remote copies, remote signals or barrier semaphores. Data moves between devices by JAX's collectives and lax.ppermute only.
A program may use at most 192 MiB of HBM per device.

```python
import math
import jax
import jax.numpy as jnp
from jax import lax

D = 1792
HEAD_DIM = 112
HEADS = 8
HW = 896
PATCHES = 256
SLOTS = 4
IMAGES = 64
N_SECTION = 16
N_REP = 8


def draw_counts(key, part):
    key = jax.random.fold_in(key, 11)
    first, second, third = jax.random.split(key, 3)
    base = jax.random.randint(first, (N_REP, N_SECTION), 0, 3)
    bumps = jax.random.randint(second, (N_REP, N_SECTION), 0, 8)
    base = base + 2 * (bumps == 0).astype(jnp.int32)
    chosen = jax.random.randint(third, (N_REP, 1), 0, N_SECTION)
    base = jnp.where(jnp.arange(N_SECTION)[None, :] == chosen, 4, base)
    return jnp.minimum(base, SLOTS).astype(jnp.int32)


def draw_patches(key, part):
    key = jax.random.fold_in(key, 12)
    first, second, third = jax.random.split(key, 3)
    shape = (N_REP, IMAGES, PATCHES, D)
    base = jnp.clip(jax.random.normal(first, shape, jnp.float32), -5.0, 5.0)
    rows = jnp.exp(jax.random.uniform(second, (N_REP, IMAGES, PATCHES, 1), jnp.float32, math.log(0.5), math.log(2.0)))
    columns = jnp.exp(jax.random.uniform(third, (D,), jnp.float32, math.log(0.3), math.log(3.0)))
    return (base * rows * columns).astype(jnp.bfloat16)


def draw_w_qkv(key, part):
    key = jax.random.fold_in(key, 13)
    first = jax.random.fold_in(key, 0)
    width = HEADS * HEAD_DIM
    whole = jnp.clip(jax.random.normal(first, (D, 3 * width), jnp.float32), -5.0, 5.0) / D ** 0.5
    return whole.astype(jnp.bfloat16)


def steps_of(stream_key, dims, shards, smallest, largest):
    level = 1.0
    for position, blocks in shards:
        heights = jax.random.uniform(jax.random.fold_in(jax.random.fold_in(stream_key, 6), position), (blocks,), jnp.float32, smallest / len(shards), largest / len(shards))
        level = level * jnp.repeat(jnp.exp(heights), dims[position] // blocks).reshape((-1,) + (1,) * (len(dims) - 1 - position))
    return level


def centred(key, dims, scale, most, pieces=(), held_as=jnp.bfloat16):
    values = jax.random.normal(key, dims, jnp.float32) * scale
    if len(pieces) > 0:
        values = steps_of(key, dims, pieces, -0.22, 0.18) * values
    return jnp.clip(values, min=-most, max=most).astype(held_as)


def setup_inputs(seed: int = 0) -> dict:
    seeds = jax.random.split(jax.random.key(seed), 6)
    patches = draw_patches(jax.random.fold_in(seeds[5], 71), 0)
    counts = draw_counts(jax.random.fold_in(seeds[5], 71), 0)
    gain = jnp.clip(1.0 + 0.1 * jax.random.normal(seeds[2], (D,), jnp.float32), 0.5, 1.5)
    w_qkv = draw_w_qkv(jax.random.fold_in(seeds[5], 71), 0)
    cotangent = centred(seeds[4], (N_REP, IMAGES, PATCHES, HW), 0.01, 0.0625, ((0, 8), (1, 16)))
    return dict(patches=patches, counts=counts, gain=gain, w_qkv=w_qkv, cotangent=cotangent)


def layer_normalize(hidden_input, gain):
    xf = hidden_input.astype(jnp.float32)
    mean_removed = xf - lax.optimization_barrier(jnp.mean(xf, -1, keepdims=True))
    inverse_deviation = lax.optimization_barrier(jnp.mean(mean_removed * mean_removed, -1, keepdims=True))
    standardized_input = mean_removed * lax.rsqrt(inverse_deviation + 1e-06)
    return (standardized_input, (standardized_input * gain).astype(jnp.bfloat16))

def split_heads(qkv):
    rows = qkv.shape[0]
    width = qkv.shape[1] // 3
    query = qkv[:, :width].reshape(rows, HEADS, HEAD_DIM).astype(jnp.float32)
    keys = qkv[:, width:2 * width].reshape(rows, HEADS, HEAD_DIM).astype(jnp.float32)
    values = qkv[:, 2 * width:].reshape(rows, HEADS, HEAD_DIM).astype(jnp.float32)
    return (query, keys, values)

def softmax_probs(query, keys):
    scores = jnp.einsum('phe,qhe->hpq', query, keys) * HEAD_DIM ** (-0.5)
    top = lax.optimization_barrier(jnp.max(scores, -1, keepdims=True))
    weights = jnp.exp(scores - top)
    return weights / lax.optimization_barrier(jnp.sum(weights, -1, keepdims=True))

def image_pass(hidden_input, gain, w_qkv, grad_out):
    rows = hidden_input.shape[0]
    standardized_input, normalized_rows = layer_normalize(hidden_input, gain)
    qkv = jnp.dot(normalized_rows, w_qkv, preferred_element_type=jnp.float32).astype(jnp.bfloat16)
    query, keys, values = split_heads(qkv)
    probs = softmax_probs(query, keys)
    probs_low = probs.astype(jnp.bfloat16).astype(jnp.float32)
    mixed = jnp.einsum('hpq,qhe->phe', probs_low, values).astype(jnp.bfloat16).reshape(rows, -1)
    upstream = grad_out.astype(jnp.float32).reshape(rows, HEADS, HEAD_DIM)
    grad_values = jnp.einsum('hpq,phe->qhe', probs_low, upstream)
    grad_probs = jnp.einsum('phe,qhe->hpq', upstream, values)
    inner = lax.optimization_barrier(jnp.sum(probs * grad_probs, -1, keepdims=True))
    grad_scores = (probs * (grad_probs - inner) * HEAD_DIM ** (-0.5)).astype(jnp.bfloat16).astype(jnp.float32)
    grad_query = jnp.einsum('hpq,qhe->phe', grad_scores, keys)
    grad_keys = jnp.einsum('hpq,phe->qhe', grad_scores, query)
    gradient_query_key_value = jnp.concatenate([grad_query.reshape(rows, -1), grad_keys.reshape(rows, -1), grad_values.reshape(rows, -1)], 1).astype(jnp.bfloat16)
    gradient_normalized = jnp.einsum('pc,dc->pd', gradient_query_key_value.astype(jnp.float32), w_qkv.astype(jnp.float32))
    gain_product = lax.optimization_barrier(jnp.sum(gradient_normalized * standardized_input, 0))
    weight_term = jnp.einsum('pd,pc->dc', normalized_rows.astype(jnp.float32), gradient_query_key_value.astype(jnp.float32))
    return (mixed, weight_term, gain_product)

def reference(patches, counts, gain, w_qkv, cotangent):
    before = (jnp.cumsum(counts, axis=1, dtype=jnp.int32) - counts).astype(jnp.int32)
    width = w_qkv.shape[1] // 3
    total_slots = N_REP * N_SECTION * SLOTS

    def step(carry, index):
        grad_w, grad_g = carry
        replica = index // (N_SECTION * SLOTS)
        device = index // SLOTS % N_SECTION
        slot = index % SLOTS
        held = counts[replica, device]
        live = slot < held
        listed = before[replica, device] + slot
        place = jnp.where(live, listed % N_SECTION * SLOTS + listed // N_SECTION, 0).astype(jnp.int32)
        hidden_input = patches[replica, device * SLOTS + slot]
        grad_out = cotangent[replica, place]

        def work(ignored_slot):
            return image_pass(hidden_input, gain, w_qkv, grad_out)

        def skip(ignored_slot):
            return (jnp.zeros((PATCHES, width), jnp.bfloat16), jnp.zeros((D, 3 * width), jnp.float32), jnp.zeros((D,), jnp.float32))
        mixed, weight_term, gain_product = lax.cond(live, work, skip, None)
        return ((grad_w + weight_term, grad_g + gain_product), (mixed, replica, place))
    start = (jnp.zeros((D, 3 * width), jnp.float32), jnp.zeros((D,), jnp.float32))
    (gradient_query_key_value, grad_gain), (mixed_all, replicas, places) = lax.scan(step, start, jnp.arange(total_slots, dtype=jnp.int32))
    encoded = jnp.zeros((N_REP, IMAGES, PATCHES, width), jnp.bfloat16).at[replicas, places].add(mixed_all)
    return (encoded, gradient_query_key_value, grad_gain)
```

```python
import jax
import jax.numpy as jnp
import numpy as np
from jax import lax
from jax.experimental import pallas as pl
from jax.experimental.pallas import tpu as pltpu
from jax.sharding import PartitionSpec as P

D = 1792
E = 112
HEADS = 8
LOCAL = 4
HALF = LOCAL * E
PATCH = 256
SLOTS = 4
IMAGES = 8
ROWS = 3 * HALF
PAR = D // 2
F32 = jnp.float32
BF = jnp.bfloat16
SCALE = E ** (-0.5)

ZHEADS = np.array(
    [
        [[0, 1, 2], [3, 8, 9], [4, 10, 11], [5, 6, 7]],
        [[4, 5, 6], [0, 1, 7], [2, 3, 8], [9, 10, 11]],
    ],
    np.int32,
)
FINAL = np.array(
    [
        [[0, 1, 2], [3, 4, 5]],
        [[0, 3, 4], [5, 1, 2]],
        [[3, 4, 0], [1, 2, 5]],
        [[0, 1, 2], [3, 4, 5]],
    ],
    np.int32,
)


def section_index(x, y, core):
    return x * 4 + y * 2 + core


CORE_SWAP = [(i, i ^ 1) for i in range(16)]
PLANES = [
    [section_index(x, yl, core) * 8 + yh * 4 + z for x in range(4) for yh in range(2) for yl in range(2)]
    for z in range(4)
    for core in range(2)
]


def z_moves(steps):
    pairs = []
    for chip in range(8):
        for core_from, step, core_to in steps:
            for yh in range(2):
                for z in range(4):
                    pairs.append(
                        (
                            (chip * 2 + core_from) * 8 + yh * 4 + z,
                            (chip * 2 + core_to) * 8 + yh * 4 + (z + step) % 4,
                        )
                    )
    return pairs


Z_SAME_OUT = z_moves([(0, 1, 0), (1, -1, 1)])
Z_CROSS_OUT = z_moves([(0, 1, 1), (1, -1, 0)])
Z_SAME_BACK = z_moves([(0, -1, 0), (1, 1, 1)])


def params(mib=60):
    return pltpu.CompilerParams(vmem_limit_bytes=mib * 1024 * 1024)


def turned(value):
    return value.astype(F32).T.astype(BF)


def weights_kernel(meta, w_ref, out_ref):
    for core in range(2):

        @pl.when(meta[0] == core)
        def _():
            for kind in range(3):
                start = kind * HEADS * E + core * HALF
                out_ref[kind * HALF : (kind + 1) * HALF, :] = turned(w_ref[:, start : start + HALF])


def turn_weights(core, w):
    return pl.pallas_call(
        weights_kernel,
        grid_spec=pltpu.PrefetchScalarGridSpec(
            num_scalar_prefetch=1,
            grid=(D // 256,),
            in_specs=[pl.BlockSpec((256, 3 * HEADS * E), lambda i, m: (i, 0))],
            out_specs=pl.BlockSpec((ROWS, 256), lambda i, m: (0, i)),
        ),
        out_shape=jax.ShapeDtypeStruct((ROWS, D), BF),
        compiler_params=params(),
        name="turn_weights",
    )(core.reshape(1), w)


def cot_kernel(meta, cot_ref, out_ref):
    chip = pl.program_id(0)

    @pl.when(meta[8 + chip] == 1)
    def _():
        both = turned(cot_ref[0])
        out_ref[0] = both[:HALF]
        out_ref[1] = both[HALF:]


def pick_cotangent(meta, cot):
    return pl.pallas_call(
        cot_kernel,
        grid_spec=pltpu.PrefetchScalarGridSpec(
            num_scalar_prefetch=1,
            grid=(8,),
            in_specs=[pl.BlockSpec((1, PATCH, 2 * HALF), lambda i, m: (m[i], 0, 0))],
            out_specs=pl.BlockSpec((2, HALF, PATCH), lambda i, m: (i, 0, 0)),
        ),
        out_shape=jax.ShapeDtypeStruct((16, HALF, PATCH), BF),
        compiler_params=params(),
        name="pick_cotangent",
    )(meta, cot)


def forward_kernel(meta, own_ref, sib_ref, gain_ref, wt_ref, normed_ref, qkv_ref, probs_ref, enc_ref):
    image = pl.program_id(0)
    count = meta[0]

    @pl.when(image == count)
    def _():
        normed_ref[...] = jnp.zeros_like(normed_ref)

    @pl.when(image < count)
    def _():
        from_own = meta[8 + image] == 1
        chunk = 32
        for start in range(0, PATCH, chunk):
            rows = slice(start, start + chunk)
            xf = jnp.where(from_own, own_ref[0, rows, :], sib_ref[0, rows, :]).astype(F32)
            centred = xf - jnp.sum(xf, -1, keepdims=True) * (1.0 / D)
            variance = jnp.sum(centred * centred, -1, keepdims=True) * (1.0 / D)
            xhat = centred * lax.rsqrt(variance + 1e-06)
            normed_ref[rows, :] = (xhat * gain_ref[...]).astype(BF)
        normed = normed_ref[...]
        qkv_ref[0] = lax.dot_general(
            wt_ref[...], normed, (((1,), (1,)), ((), ())), preferred_element_type=F32
        ).astype(BF)
        for head in range(LOCAL):
            q_t = qkv_ref[0, head * E : (head + 1) * E, :]
            k_t = qkv_ref[0, HALF + head * E : HALF + (head + 1) * E, :]
            v_t = qkv_ref[0, 2 * HALF + head * E : 2 * HALF + (head + 1) * E, :]
            scores = jnp.dot(turned(k_t), q_t, preferred_element_type=F32) * SCALE
            weights = jnp.exp(scores - jnp.max(scores, 0, keepdims=True))
            probs = weights * (1.0 / jnp.sum(weights, 0, keepdims=True))
            probs_ref[0, head] = probs
            enc_ref[0, head * E : (head + 1) * E, :] = jnp.dot(
                v_t, probs.astype(BF), preferred_element_type=F32
            ).astype(BF)


def run_forward(meta, own, sib, gain, wt):
    def last(i, m):
        return jnp.minimum(i, m[1])

    return pl.pallas_call(
        forward_kernel,
        grid_spec=pltpu.PrefetchScalarGridSpec(
            num_scalar_prefetch=1,
            grid=(IMAGES,),
            in_specs=[
                pl.BlockSpec((1, PATCH, D), lambda i, m: (m[16 + i], 0, 0)),
                pl.BlockSpec((1, PATCH, D), lambda i, m: (m[24 + i], 0, 0)),
                pl.BlockSpec((1, D), lambda i, m: (0, 0)),
                pl.BlockSpec((ROWS, D), lambda i, m: (0, 0)),
            ],
            out_specs=[
                pl.BlockSpec((PATCH, D), lambda i, m: (jnp.minimum(jnp.minimum(i, m[0]), 7), 0)),
                pl.BlockSpec((1, ROWS, PATCH), lambda i, m: (last(i, m), 0, 0)),
                pl.BlockSpec((1, LOCAL, PATCH, PATCH), lambda i, m: (last(i, m), 0, 0, 0)),
                pl.BlockSpec((1, HALF, PATCH), lambda i, m: (m[32 + last(i, m)], 0, 0)),
            ],
        ),
        out_shape=[
            jax.ShapeDtypeStruct((IMAGES * PATCH, D), BF),
            jax.ShapeDtypeStruct((IMAGES, ROWS, PATCH), BF),
            jax.ShapeDtypeStruct((IMAGES, LOCAL, PATCH, PATCH), F32),
            jax.ShapeDtypeStruct((16, HALF, PATCH), BF),
        ],
        compiler_params=params(),
        cost_estimate=pl.CostEstimate(flops=20 * 10**9, bytes_accessed=30 * 10**6, transcendentals=0),
        name="forward",
    )(meta, own, sib, gain.reshape(1, D), wt)


def parity_parts(block):
    return [
        jnp.concatenate(
            [block[:, (2 * i + parity) * E : (2 * i + parity + 1) * E] for i in range(8)], axis=1
        ).astype(BF)
        for parity in range(2)
    ]


def backward_kernel(
    meta, qkv_ref, probs_ref, cot_ref, normed_ref, wt_ref, grads_ref, same_ref, cross_ref, gain_ref, acc_ref
):
    image = pl.program_id(0)
    count = meta[0]

    @pl.when(image == 0)
    def _():
        acc_ref[...] = jnp.zeros_like(acc_ref)

    @pl.when(image == count)
    def _():
        grads_ref[...] = jnp.zeros_like(grads_ref)

    @pl.when(image < count)
    def _():
        for head in range(LOCAL):
            q_t = qkv_ref[0, head * E : (head + 1) * E, :]
            k_t = qkv_ref[0, HALF + head * E : HALF + (head + 1) * E, :]
            v_t = qkv_ref[0, 2 * HALF + head * E : 2 * HALF + (head + 1) * E, :]
            g_t = cot_ref[0, head * E : (head + 1) * E, :]
            probs = probs_ref[0, head]
            grad_probs = jnp.dot(turned(v_t), g_t, preferred_element_type=F32)
            inner = jnp.sum(probs * grad_probs, 0, keepdims=True)
            grad_scores = (probs * (grad_probs - inner) * SCALE).astype(BF)
            nt = (((1,), (1,)), ((), ()))
            grads_ref[head] = jnp.dot(k_t, grad_scores, preferred_element_type=F32).astype(BF)
            grads_ref[LOCAL + head] = lax.dot_general(
                q_t, grad_scores, nt, preferred_element_type=F32
            ).astype(BF)
            grads_ref[2 * LOCAL + head] = lax.dot_general(
                g_t, probs.astype(BF), nt, preferred_element_type=F32
            ).astype(BF)
        left = jnp.concatenate([grads_ref[meta[40 + t]] for t in range(3)], axis=0)
        acc_ref[...] += jnp.dot(left, normed_ref[...], preferred_element_type=F32)

    @pl.when(image == IMAGES - 1)
    def _():
        for t in range(3):
            block = acc_ref[t * E : (t + 1) * E, :]
            part = jnp.sum(wt_ref[meta[40 + t]].astype(F32) * block, 0, keepdims=True)
            if t == 0:
                gain_ref[...] = part
            else:
                gain_ref[...] += part
            even, odd = parity_parts(block)
            first = meta[2] == 0
            same_ref[t * E : (t + 1) * E, :] = jnp.where(first, even, odd)
            cross_ref[t * E : (t + 1) * E, :] = jnp.where(first, odd, even)


def run_backward(meta, qkv, probs, cot, normed, wt):
    def last(i, m):
        return jnp.minimum(i, m[1])

    return pl.pallas_call(
        backward_kernel,
        grid_spec=pltpu.PrefetchScalarGridSpec(
            num_scalar_prefetch=1,
            grid=(IMAGES,),
            in_specs=[
                pl.BlockSpec((1, ROWS, PATCH), lambda i, m: (last(i, m), 0, 0)),
                pl.BlockSpec((1, LOCAL, PATCH, PATCH), lambda i, m: (last(i, m), 0, 0, 0)),
                pl.BlockSpec((1, HALF, PATCH), lambda i, m: (m[32 + last(i, m)], 0, 0)),
                pl.BlockSpec((PATCH, D), lambda i, m: (last(i, m), 0)),
                pl.BlockSpec((3 * LOCAL, E, D), lambda i, m: (0, 0, 0)),
            ],
            out_specs=[
                pl.BlockSpec(
                    (3 * LOCAL, E, PATCH), lambda i, m: (0, 0, jnp.minimum(jnp.minimum(i, m[0]), 7))
                ),
                pl.BlockSpec((3 * E, PAR), lambda i, m: (0, 0)),
                pl.BlockSpec((3 * E, PAR), lambda i, m: (0, 0)),
                pl.BlockSpec((1, D), lambda i, m: (0, 0)),
            ],
            scratch_shapes=[pltpu.VMEM((3 * E, D), F32)],
        ),
        out_shape=[
            jax.ShapeDtypeStruct((3 * LOCAL, E, IMAGES * PATCH), BF),
            jax.ShapeDtypeStruct((3 * E, PAR), BF),
            jax.ShapeDtypeStruct((3 * E, PAR), BF),
            jax.ShapeDtypeStruct((1, D), F32),
        ],
        compiler_params=params(),
        cost_estimate=pl.CostEstimate(flops=20 * 10**9, bytes_accessed=30 * 10**6, transcendentals=0),
        name="backward",
    )(meta, qkv, probs, cot, normed, wt)


def weight_kernel(meta, grads_ref, normed_ref, wt_ref, *outs):
    same, cross, gain_ref, acc_ref = outs[:3], outs[3:6], outs[6], outs[7]
    pair = pl.program_id(0)

    @pl.when(pair == 0)
    def _():
        acc_ref[...] = jnp.zeros_like(acc_ref)

    @pl.when(2 * pair < meta[0])
    def _():
        left = jnp.concatenate([grads_ref[meta[43 + t]] for t in range(9)], axis=0)
        acc_ref[...] += jnp.dot(left, normed_ref[...], preferred_element_type=F32)

    @pl.when(pair == IMAGES // 2 - 1)
    def _():
        first = meta[2] == 0
        for t in range(9):
            block = acc_ref[t * E : (t + 1) * E, :]
            part = jnp.sum(wt_ref[meta[43 + t]].astype(F32) * block, 0, keepdims=True)
            if t == 0:
                gain_ref[...] = part
            else:
                gain_ref[...] += part
            even, odd = parity_parts(block)
            rows = slice((t % 3) * E, (t % 3 + 1) * E)
            same[t // 3][rows, :] = jnp.where(first, even, odd)
            cross[t // 3][rows, :] = jnp.where(first, odd, even)


def run_weight(meta, grads, normed, wt):
    def at(i, m):
        return jnp.minimum(i, m[3])

    part = jax.ShapeDtypeStruct((3 * E, PAR), BF)
    outs = pl.pallas_call(
        weight_kernel,
        grid_spec=pltpu.PrefetchScalarGridSpec(
            num_scalar_prefetch=1,
            grid=(IMAGES // 2,),
            in_specs=[
                pl.BlockSpec((3 * LOCAL, E, 2 * PATCH), lambda i, m: (0, 0, at(i, m))),
                pl.BlockSpec((2 * PATCH, D), lambda i, m: (at(i, m), 0)),
                pl.BlockSpec((3 * LOCAL, E, D), lambda i, m: (0, 0, 0)),
            ],
            out_specs=[pl.BlockSpec((3 * E, PAR), lambda i, m: (0, 0))] * 6
            + [pl.BlockSpec((1, D), lambda i, m: (0, 0))],
            scratch_shapes=[pltpu.VMEM((9 * E, D), F32)],
        ),
        out_shape=[part] * 6 + [jax.ShapeDtypeStruct((1, D), F32)],
        compiler_params=params(),
        cost_estimate=pl.CostEstimate(flops=10 * 10**9, bytes_accessed=20 * 10**6, transcendentals=0),
        name="weight_gradient",
    )(meta, grads, normed, wt)
    return outs[:3], outs[3:6], outs[6]


def gather_kernel(meta, own_ref, sib_ref, a0, a1, b0, b1, out_ref, sum_ref):
    mine = own_ref[...].astype(F32) + a0[...].astype(F32) + b0[...].astype(F32)
    other = sib_ref[...].astype(F32) + a1[...].astype(F32) + b1[...].astype(F32)
    for t in range(3):
        sum_ref[t, :E, :] = mine[t * E : (t + 1) * E]
        sum_ref[3 + t, :E, :] = other[t * E : (t + 1) * E]
    for t in range(6):
        flipped = sum_ref[meta[1 + t]].T.astype(BF)
        yh, column = t // 3, t % 3
        for x in range(4):
            for yl in range(2):
                row = (x * 2 + yl) * E
                out_ref[(x * 2 + yh) * 2 + yl, :, column * 128 : (column + 1) * 128] = flipped[
                    row : row + E
                ]


def gather_blocks(meta, *parts):
    whole = pl.BlockSpec((3 * E, PAR), lambda i, m: (0, 0))
    return pl.pallas_call(
        gather_kernel,
        grid_spec=pltpu.PrefetchScalarGridSpec(
            num_scalar_prefetch=1,
            grid=(1,),
            in_specs=[whole] * 6,
            out_specs=pl.BlockSpec((16, E, 384), lambda i, m: (0, 0, 0)),
            scratch_shapes=[pltpu.VMEM((6, 128, PAR), F32)],
        ),
        out_shape=jax.ShapeDtypeStruct((16, E, 384), BF),
        compiler_params=params(),
        name="gather_blocks",
    )(meta, *parts)


def final_kernel(in_ref, out_ref):
    total = in_ref[0].astype(F32)
    for i in range(1, 16):
        total += in_ref[i].astype(F32)
    out_ref[...] = jnp.concatenate([total[:, t * 128 : t * 128 + E] for t in range(3)], axis=1)


def final_sum(blocks):
    return pl.pallas_call(
        final_kernel,
        out_shape=jax.ShapeDtypeStruct((E, 3 * E), F32),
        compiler_params=params(),
        name="final_sum",
    )(blocks)


def place_kernel(meta, in_ref, out_ref):
    slot = pl.program_id(0)

    @pl.when(meta[8 + slot] == 1)
    def _():
        out_ref[0, :, :] = turned(in_ref[...].reshape(2 * HALF, PATCH))

    @pl.when(meta[8 + slot] == 0)
    def _():
        out_ref[...] = jnp.zeros_like(out_ref)


def place_encoded(meta, arrived):
    return pl.pallas_call(
        place_kernel,
        grid_spec=pltpu.PrefetchScalarGridSpec(
            num_scalar_prefetch=1,
            grid=(SLOTS,),
            in_specs=[pl.BlockSpec((2, HALF, PATCH), lambda i, m: (m[i], 0, 0))],
            out_specs=pl.BlockSpec((1, PATCH, 2 * HALF), lambda i, m: (i, 0, 0)),
        ),
        out_shape=jax.ShapeDtypeStruct((SLOTS, PATCH, 2 * HALF), BF),
        compiler_params=params(),
        name="place_encoded",
    )(meta, arrived)


def per_device(patches, counts, gain, w_qkv, cotangent):
    me = lax.axis_index("section")
    core, chip = me % 2, me // 2
    z = lax.axis_index("rep") % 4
    i32 = jnp.int32

    sibling = lax.ppermute(patches[0], "section", CORE_SWAP)
    wt = turn_weights(core.astype(i32), w_qkv)
    every = lax.all_gather(counts, "section", axis=1, tiled=True)[0]

    held = jnp.sum(every.reshape(8, 2), 1)
    start = jnp.cumsum(held, dtype=i32) - held
    total = jnp.sum(held)
    chips = jnp.arange(8, dtype=i32)
    is_me = chips == chip
    count = jnp.sum(jnp.where(is_me, held, 0))
    begin = jnp.sum(jnp.where(is_me, start, 0))
    first_core = jnp.sum(jnp.where(jnp.arange(16) == 2 * chip, every, 0))
    own_count = counts[0, 0]
    sib_count = count - own_count
    order = jnp.arange(8, dtype=i32)
    own_start = jnp.where(core == 0, 0, first_core)
    sib_start = jnp.where(core == 0, first_core, 0)
    own_slot = jnp.clip(order - own_start, 0, jnp.maximum(own_count - 1, 0))
    sib_slot = jnp.clip(order - sib_start, 0, jnp.maximum(sib_count - 1, 0))
    from_own = ((order < first_core) == (core == 0)).astype(i32)
    target = (begin + order) % 16
    last = jnp.maximum(count - 1, 0)
    table = jnp.asarray(ZHEADS)[core]
    first_z = jnp.where(core == 0, (z + 1) % 4, (z + 3) % 4)
    second_z = jnp.where(core == 0, (z + 3) % 4, (z + 1) % 4)
    zs = jnp.stack([(z + 2) % 4, first_z, second_z, z])
    heads = table[zs].reshape(12)
    head_part = jnp.stack(
        [count, last, core, jnp.maximum((count + 1) // 2 - 1, 0), 0 * core, 0 * core, 0 * core, 0 * core]
    ).astype(i32)
    meta = jnp.concatenate([head_part, from_own, own_slot, sib_slot, target, heads]).astype(i32)

    off = (me - start) % 16
    cot_meta = jnp.concatenate([jnp.clip((start + off) // 16, 0, SLOTS - 1), (off < held).astype(i32)])
    cot_send = pick_cotangent(cot_meta.astype(i32), cotangent[0])
    cot = lax.all_to_all(cot_send, "section", split_axis=0, concat_axis=0, tiled=True)

    normed, qkv, probs, enc_send = run_forward(meta, patches[0], sibling, gain, wt)
    cot, enc_send = lax.optimization_barrier((cot, enc_send))
    enc = lax.all_to_all(enc_send, "section", split_axis=0, concat_axis=0, tiled=True)

    wt_heads = wt.reshape(3 * LOCAL, E, D)
    grads, same, cross, gain_a = run_backward(meta, qkv, probs, cot, normed, wt_heads)
    both = ("section", "rep")
    same = lax.ppermute(same, both, Z_SAME_OUT)
    cross = lax.ppermute(cross, both, Z_CROSS_OUT)
    own, theirs, gain_b = run_weight(meta, grads, normed, wt_heads)
    sib = [lax.ppermute(part, "section", CORE_SWAP) for part in theirs]

    gain_part = (gain_a + gain_b)[0] / gain
    gain_sum = jnp.sum(
        lax.all_to_all(
            jnp.broadcast_to(gain_part, (16, D)), "section", split_axis=0, concat_axis=0, tiled=True
        ),
        0,
    )
    grad_gain = jnp.sum(
        lax.all_to_all(jnp.broadcast_to(gain_sum, (8, D)), "rep", split_axis=0, concat_axis=0, tiled=True), 0
    )

    a1 = lax.ppermute(sib[1], both, Z_SAME_OUT)
    b0 = lax.ppermute(own[1], both, Z_SAME_BACK)
    a0 = lax.ppermute(own[0] + same, both, Z_SAME_OUT)
    b1 = lax.ppermute(sib[0] + cross, both, Z_SAME_BACK)

    pick = jnp.asarray(FINAL)[z].reshape(6)
    pick = jnp.where(core == 0, pick, (pick + 3) % 6)
    blocks = gather_blocks(
        jnp.concatenate([core.reshape(1), pick]).astype(i32), own[2], sib[2], a0, a1, b0, b1
    )
    arrived = lax.all_to_all(
        blocks, both, split_axis=0, concat_axis=0, tiled=True, axis_index_groups=PLANES
    )
    grad_block = final_sum(arrived)

    places = me + 16 * jnp.arange(SLOTS, dtype=i32)
    holder = jnp.sum((start[None, :] + held[None, :] <= places[:, None]).astype(i32), 1)
    place_meta = jnp.concatenate(
        [jnp.clip(holder, 0, 7), jnp.zeros((4,), i32), (places < total).astype(i32)]
    )
    encoded = place_encoded(place_meta.astype(i32), enc)
    return (encoded[None], grad_block, grad_gain)


def solution(mesh):
    return jax.shard_map(
        per_device,
        mesh=mesh,
        in_specs=(
            P("rep", "section", None, None),
            P("rep", "section"),
            P(),
            P(),
            P("rep", "section", None, None),
        ),
        out_specs=(P("rep", "section", None, None), P("section", "rep"), P()),
        check_vma=False,
    )
```

```python
import jax
import jax.numpy as jnp
import numpy as np
from jax import lax
from jax.experimental import pallas as pl
from jax.experimental.pallas import tpu as pltpu
from jax.sharding import PartitionSpec as P

D = 1792
E = 112
HEADS = 8
LOCAL = 4
HALF = LOCAL * E
PATCH = 256
SLOTS = 4
IMAGES = 8
ROWS = 3 * HALF
PAR = D // 2
F32 = jnp.float32
BF = jnp.bfloat16
SCALE = E ** (-0.5)

ZHEADS = np.array(
    [
        [[0, 1, 2], [3, 8, 9], [4, 10, 11], [5, 6, 7]],
        [[4, 5, 6], [0, 1, 7], [2, 3, 8], [9, 10, 11]],
    ],
    np.int32,
)
FINAL = np.array(
    [
        [[0, 1, 2], [3, 4, 5]],
        [[0, 3, 4], [5, 1, 2]],
        [[3, 4, 0], [1, 2, 5]],
        [[0, 1, 2], [3, 4, 5]],
    ],
    np.int32,
)


def section_index(x, y, core):
    return x * 4 + y * 2 + core


CORE_SWAP = [(i, i ^ 1) for i in range(16)]
PLANES = [
    [section_index(x, yl, core) * 8 + yh * 4 + z for x in range(4) for yh in range(2) for yl in range(2)]
    for z in range(4)
    for core in range(2)
]


def z_moves(steps):
    pairs = []
    for chip in range(8):
        for core_from, step, core_to in steps:
            for yh in range(2):
                for z in range(4):
                    pairs.append(
                        (
                            (chip * 2 + core_from) * 8 + yh * 4 + z,
                            (chip * 2 + core_to) * 8 + yh * 4 + (z + step) % 4,
                        )
                    )
    return pairs


Z_SAME_OUT = z_moves([(0, 1, 0), (1, -1, 1)])
Z_CROSS_OUT = z_moves([(0, 1, 1), (1, -1, 0)])
Z_SAME_BACK = z_moves([(0, -1, 0), (1, 1, 1)])
Z_CROSS_BACK = z_moves([(0, -1, 1), (1, 1, 0)])
Z_TURNS = [[(i, i // 4 * 4 + (i + step) % 4) for i in range(8)] for step in (1, 2, 3)]


def params(mib=60):
    return pltpu.CompilerParams(vmem_limit_bytes=mib * 1024 * 1024)


def turned(value):
    return value.astype(F32).T.astype(BF)


def weights_kernel(meta, w_ref, out_ref):
    rows = lax.broadcasted_iota(jnp.int32, (HALF, HALF), 0)
    unit = (rows == lax.broadcasted_iota(jnp.int32, (HALF, HALF), 1)).astype(F32).astype(BF)
    for core in range(2):

        @pl.when(meta[0] == core)
        def _():
            for kind in range(3):
                start = kind * HEADS * E + core * HALF
                out_ref[kind * HALF : (kind + 1) * HALF, :] = lax.dot_general(
                    unit, w_ref[:, start : start + HALF], (((1,), (1,)), ((), ())), preferred_element_type=F32
                ).astype(BF)


def turn_weights(core, w):
    return pl.pallas_call(
        weights_kernel,
        grid_spec=pltpu.PrefetchScalarGridSpec(
            num_scalar_prefetch=1,
            grid=(D // 256,),
            in_specs=[pl.BlockSpec((256, 3 * HEADS * E), lambda i, m: (i, 0))],
            out_specs=pl.BlockSpec((ROWS, 256), lambda i, m: (0, i)),
        ),
        out_shape=jax.ShapeDtypeStruct((ROWS, D), BF),
        compiler_params=params(),
        name="turn_weights",
    )(core.reshape(1), w)


def turn_kernel(cot_ref, out_ref):
    both = turned(cot_ref[0])
    out_ref[0, 0] = both[:HALF]
    out_ref[0, 1] = both[HALF:]


def turn_cotangent(cot):
    return pl.pallas_call(
        turn_kernel,
        grid=(SLOTS,),
        in_specs=[pl.BlockSpec((1, PATCH, 2 * HALF), lambda i: (i, 0, 0))],
        out_specs=pl.BlockSpec((1, 2, HALF, PATCH), lambda i: (i, 0, 0, 0)),
        out_shape=jax.ShapeDtypeStruct((SLOTS, 2, HALF, PATCH), BF),
        compiler_params=params(),
        name="turn_cotangent",
    )(cot)


def pick_kernel(meta, cot_ref, out_ref, sems):
    def copy(chip):
        return pltpu.make_async_copy(
            cot_ref.at[meta[chip]], out_ref.at[pl.ds(2 * chip, 2)], sems.at[chip]
        )

    for chip in range(8):

        @pl.when(meta[8 + chip] == 1)
        def _():
            copy(chip).start()

    for chip in range(8):

        @pl.when(meta[8 + chip] == 1)
        def _():
            copy(chip).wait()


def pick_cotangent(meta, cot):
    return pl.pallas_call(
        pick_kernel,
        in_specs=[pl.BlockSpec(memory_space=pltpu.SMEM), pl.BlockSpec(memory_space=pltpu.VMEM)],
        out_specs=pl.BlockSpec(memory_space=pl.ANY),
        out_shape=jax.ShapeDtypeStruct((16, HALF, PATCH), BF),
        scratch_shapes=[pltpu.SemaphoreType.DMA((8,))],
        compiler_params=params(),
        name="pick_cotangent",
    )(meta, cot)


def forward_kernel(meta, own_ref, sib_ref, gain_ref, wt_ref, normed_ref, qkv_ref, probs_ref, enc_ref):
    image = pl.program_id(0)
    count = meta[0]

    @pl.when(image == count)
    def _():
        normed_ref[...] = jnp.zeros_like(normed_ref)

    @pl.when(image < count)
    def _():
        from_own = meta[8 + image] == 1
        chunk = 32
        for start in range(0, PATCH, chunk):
            rows = slice(start, start + chunk)
            xf = jnp.where(from_own, own_ref[0, rows, :], sib_ref[0, rows, :]).astype(F32)
            centred = xf - jnp.sum(xf, -1, keepdims=True) * (1.0 / D)
            variance = jnp.sum(centred * centred, -1, keepdims=True) * (1.0 / D)
            xhat = centred * lax.rsqrt(variance + 1e-06)
            normed_ref[rows, :] = (xhat * gain_ref[...]).astype(BF)
        normed = normed_ref[...]
        qkv_ref[0] = lax.dot_general(
            wt_ref[...], normed, (((1,), (1,)), ((), ())), preferred_element_type=F32
        ).astype(BF)
        for head in range(LOCAL):
            q_t = qkv_ref[0, head * E : (head + 1) * E, :]
            k_t = qkv_ref[0, HALF + head * E : HALF + (head + 1) * E, :]
            v_t = qkv_ref[0, 2 * HALF + head * E : 2 * HALF + (head + 1) * E, :]
            scores = jnp.dot(turned(k_t), q_t, preferred_element_type=F32) * SCALE
            weights = jnp.exp(scores - jnp.max(scores, 0, keepdims=True))
            probs = weights * (1.0 / jnp.sum(weights, 0, keepdims=True))
            probs_ref[0, head] = probs
            enc_ref[0, head * E : (head + 1) * E, :] = jnp.dot(
                v_t, probs.astype(BF), preferred_element_type=F32
            ).astype(BF)


def run_forward(meta, own, sib, gain, wt):
    def last(i, m):
        return jnp.minimum(i, m[1])

    return pl.pallas_call(
        forward_kernel,
        grid_spec=pltpu.PrefetchScalarGridSpec(
            num_scalar_prefetch=1,
            grid=(IMAGES,),
            in_specs=[
                pl.BlockSpec((1, PATCH, D), lambda i, m: (m[16 + i], 0, 0)),
                pl.BlockSpec((1, PATCH, D), lambda i, m: (m[24 + i], 0, 0)),
                pl.BlockSpec((1, D), lambda i, m: (0, 0)),
                pl.BlockSpec((ROWS, D), lambda i, m: (0, 0)),
            ],
            out_specs=[
                pl.BlockSpec((PATCH, D), lambda i, m: (jnp.minimum(jnp.minimum(i, m[0]), 7), 0)),
                pl.BlockSpec((1, ROWS, PATCH), lambda i, m: (last(i, m), 0, 0)),
                pl.BlockSpec((1, LOCAL, PATCH, PATCH), lambda i, m: (last(i, m), 0, 0, 0)),
                pl.BlockSpec((1, HALF, PATCH), lambda i, m: (m[32 + last(i, m)], 0, 0)),
            ],
        ),
        out_shape=[
            jax.ShapeDtypeStruct((IMAGES * PATCH, D), BF),
            jax.ShapeDtypeStruct((IMAGES, ROWS, PATCH), BF),
            jax.ShapeDtypeStruct((IMAGES, LOCAL, PATCH, PATCH), F32),
            jax.ShapeDtypeStruct((16, HALF, PATCH), BF),
        ],
        compiler_params=params(),
        cost_estimate=pl.CostEstimate(flops=20 * 10**9, bytes_accessed=30 * 10**6, transcendentals=0),
        name="forward",
    )(meta, own, sib, gain.reshape(1, D), wt)


def parity_parts(block, core):
    even, odd = [
        jnp.concatenate(
            [block[:, (2 * i + parity) * E : (2 * i + parity + 1) * E] for i in range(8)], axis=1
        ).astype(BF)
        for parity in range(2)
    ]
    return jnp.where(core == 0, even, odd), jnp.where(core == 0, odd, even)


def backward_kernel(
    meta, qkv_ref, probs_ref, cot_ref, normed_ref, wt_ref, grads_ref, opposite_ref, gain_ref, acc_ref
):
    image = pl.program_id(0)
    count = meta[0]

    @pl.when(image == 0)
    def _():
        acc_ref[...] = jnp.zeros_like(acc_ref)

    @pl.when(image == count)
    def _():
        grads_ref[...] = jnp.zeros_like(grads_ref)

    @pl.when(image < count)
    def _():
        for head in range(LOCAL):
            q_t = qkv_ref[0, head * E : (head + 1) * E, :]
            k_t = qkv_ref[0, HALF + head * E : HALF + (head + 1) * E, :]
            v_t = qkv_ref[0, 2 * HALF + head * E : 2 * HALF + (head + 1) * E, :]
            g_t = cot_ref[0, head * E : (head + 1) * E, :]
            probs = probs_ref[0, head]
            grad_probs = jnp.dot(turned(v_t), g_t, preferred_element_type=F32)
            inner = jnp.sum(probs * grad_probs, 0, keepdims=True)
            grad_scores = (probs * (grad_probs - inner) * SCALE).astype(BF)
            nt = (((1,), (1,)), ((), ()))
            grads_ref[head] = jnp.dot(k_t, grad_scores, preferred_element_type=F32).astype(BF)
            grads_ref[LOCAL + head] = lax.dot_general(
                q_t, grad_scores, nt, preferred_element_type=F32
            ).astype(BF)
            grads_ref[2 * LOCAL + head] = lax.dot_general(
                g_t, probs.astype(BF), nt, preferred_element_type=F32
            ).astype(BF)
        left = jnp.concatenate([grads_ref[meta[40 + t]] for t in range(3)], axis=0)
        acc_ref[...] += jnp.dot(left, normed_ref[...], preferred_element_type=F32)

    @pl.when(image == IMAGES - 1)
    def _():
        for t in range(3):
            block = acc_ref[t * E : (t + 1) * E, :]
            part = jnp.sum(wt_ref[meta[40 + t]].astype(F32) * block, 0, keepdims=True)
            if t == 0:
                gain_ref[...] = part
            else:
                gain_ref[...] += part
            same, cross = parity_parts(block, meta[2])
            opposite_ref[t * E : (t + 1) * E, :PAR] = same
            opposite_ref[t * E : (t + 1) * E, PAR:] = cross


def run_backward(meta, qkv, probs, cot, normed, wt):
    def last(i, m):
        return jnp.minimum(i, m[1])

    return pl.pallas_call(
        backward_kernel,
        grid_spec=pltpu.PrefetchScalarGridSpec(
            num_scalar_prefetch=1,
            grid=(IMAGES,),
            in_specs=[
                pl.BlockSpec((1, ROWS, PATCH), lambda i, m: (last(i, m), 0, 0)),
                pl.BlockSpec((1, LOCAL, PATCH, PATCH), lambda i, m: (last(i, m), 0, 0, 0)),
                pl.BlockSpec((1, HALF, PATCH), lambda i, m: (m[32 + last(i, m)], 0, 0)),
                pl.BlockSpec((PATCH, D), lambda i, m: (last(i, m), 0)),
                pl.BlockSpec((3 * LOCAL, E, D), lambda i, m: (0, 0, 0)),
            ],
            out_specs=[
                pl.BlockSpec(
                    (3 * LOCAL, E, PATCH), lambda i, m: (0, 0, jnp.minimum(jnp.minimum(i, m[0]), 7))
                ),
                pl.BlockSpec((3 * E, D), lambda i, m: (0, 0)),
                pl.BlockSpec((1, D), lambda i, m: (0, 0)),
            ],
            scratch_shapes=[pltpu.VMEM((3 * E, D), F32)],
        ),
        out_shape=[
            jax.ShapeDtypeStruct((3 * LOCAL, E, IMAGES * PATCH), BF),
            jax.ShapeDtypeStruct((3 * E, D), BF),
            jax.ShapeDtypeStruct((1, D), F32),
        ],
        compiler_params=params(),
        cost_estimate=pl.CostEstimate(flops=20 * 10**9, bytes_accessed=30 * 10**6, transcendentals=0),
        name="backward",
    )(meta, qkv, probs, cot, normed, wt)


def weight_kernel(
    meta, grads_ref, normed_ref, wt_ref, part_ref, scale_ref,
    first_ref, same1, cross1, same2, cross2, gain_ref, acc_ref,
):
    pair = pl.program_id(0)

    @pl.when(pair == 0)
    def _():
        acc_ref[...] = jnp.zeros_like(acc_ref)

    @pl.when(2 * pair < meta[0])
    def _():
        left = jnp.concatenate([grads_ref[meta[43 + t]] for t in range(9)], axis=0)
        acc_ref[...] += jnp.dot(left, normed_ref[...], preferred_element_type=F32)

    @pl.when(pair == IMAGES // 2 - 1)
    def _():
        total = part_ref[...]
        for t in range(9):
            block = acc_ref[t * E : (t + 1) * E, :]
            total += jnp.sum(wt_ref[meta[43 + t]].astype(F32) * block, 0, keepdims=True)
            same, cross = parity_parts(block, meta[2])
            rows = slice((t % 3) * E, (t % 3 + 1) * E)
            if t < 3:
                first_ref[rows, :PAR] = same
                first_ref[rows, PAR:] = cross
            else:
                (same1, same2)[t // 3 - 1][rows, :] = same
                (cross1, cross2)[t // 3 - 1][rows, :] = cross
        gain_ref[...] = total / scale_ref[...]


def run_weight(meta, grads, normed, wt, gain_part, gain):
    def at(i, m):
        return jnp.minimum(i, m[3])

    part = jax.ShapeDtypeStruct((3 * E, PAR), BF)
    row = pl.BlockSpec((1, D), lambda i, m: (0, 0))
    return pl.pallas_call(
        weight_kernel,
        grid_spec=pltpu.PrefetchScalarGridSpec(
            num_scalar_prefetch=1,
            grid=(IMAGES // 2,),
            in_specs=[
                pl.BlockSpec((3 * LOCAL, E, 2 * PATCH), lambda i, m: (0, 0, at(i, m))),
                pl.BlockSpec((2 * PATCH, D), lambda i, m: (at(i, m), 0)),
                pl.BlockSpec((3 * LOCAL, E, D), lambda i, m: (0, 0, 0)),
                row,
                row,
            ],
            out_specs=[pl.BlockSpec((3 * E, D), lambda i, m: (0, 0))]
            + [pl.BlockSpec((3 * E, PAR), lambda i, m: (0, 0))] * 4
            + [row],
            scratch_shapes=[pltpu.VMEM((9 * E, D), F32)],
        ),
        out_shape=[jax.ShapeDtypeStruct((3 * E, D), BF)] + [part] * 4 + [jax.ShapeDtypeStruct((1, D), F32)],
        compiler_params=params(),
        cost_estimate=pl.CostEstimate(flops=10 * 10**9, bytes_accessed=20 * 10**6, transcendentals=0),
        name="weight_gradient",
    )(meta, grads, normed, wt, gain_part, gain.reshape(1, D))


def gather_kernel(meta, own_ref, sib_ref, a0, a1, b0, b1, g0, g1, g2, g3, out_ref, sum_ref):
    mine = own_ref[...].astype(F32) + a0[...].astype(F32) + b0[...].astype(F32)
    other = sib_ref[...].astype(F32) + a1[...].astype(F32) + b1[...].astype(F32)
    for t in range(3):
        sum_ref[t, :E, :] = mine[t * E : (t + 1) * E]
        sum_ref[3 + t, :E, :] = other[t * E : (t + 1) * E]
    for t in range(6):
        flipped = sum_ref[meta[1 + t]].T.astype(BF)
        yh, column = t // 3, t % 3
        for x in range(4):
            for yl in range(2):
                row = (x * 2 + yl) * E
                out_ref[(x * 2 + yh) * 2 + yl, :, column * 128 : (column + 1) * 128] = flipped[
                    row : row + E
                ]
    terms = (g0[...] + g2[...]) + (g1[...] + g3[...])
    high = terms.astype(BF)
    low = (terms - high.astype(F32)).astype(BF)
    for block in range(16):
        out_ref[block, :, E:128] = high
        out_ref[block, :, 128 + E : 256] = low


def gather_blocks(meta, *parts):
    whole = pl.BlockSpec((3 * E, PAR), lambda i, m: (0, 0))
    return pl.pallas_call(
        gather_kernel,
        grid_spec=pltpu.PrefetchScalarGridSpec(
            num_scalar_prefetch=1,
            grid=(1,),
            in_specs=[whole] * 6 + [pl.BlockSpec((E, 16), lambda i, m: (0, 0))] * 4,
            out_specs=pl.BlockSpec((16, E, 384), lambda i, m: (0, 0, 0)),
            scratch_shapes=[pltpu.VMEM((6, 128, PAR), F32)],
        ),
        out_shape=jax.ShapeDtypeStruct((16, E, 384), BF),
        compiler_params=params(),
        name="gather_blocks",
    )(meta, *parts)


def final_kernel(in_ref, out_ref, gain_ref):
    total = in_ref[0].astype(F32)
    for i in range(1, 16):
        total += in_ref[i].astype(F32)
    out_ref[...] = jnp.concatenate([total[:, t * 128 : t * 128 + E] for t in range(3)], axis=1)
    gain_ref[...] = total[:, E:128] + total[:, 128 + E : 256]


def final_sum(blocks):
    return pl.pallas_call(
        final_kernel,
        out_shape=[jax.ShapeDtypeStruct((E, 3 * E), F32), jax.ShapeDtypeStruct((E, 16), F32)],
        compiler_params=params(),
        name="final_sum",
    )(blocks)


def place_kernel(meta, in_ref, out_ref):
    slot = pl.program_id(0)

    @pl.when(meta[8 + slot] == 1)
    def _():
        out_ref[0, :, :] = turned(in_ref[...].reshape(2 * HALF, PATCH))

    @pl.when(meta[8 + slot] == 0)
    def _():
        out_ref[...] = jnp.zeros_like(out_ref)


def place_encoded(meta, arrived):
    return pl.pallas_call(
        place_kernel,
        grid_spec=pltpu.PrefetchScalarGridSpec(
            num_scalar_prefetch=1,
            grid=(SLOTS,),
            in_specs=[pl.BlockSpec((2, HALF, PATCH), lambda i, m: (m[i], 0, 0))],
            out_specs=pl.BlockSpec((1, PATCH, 2 * HALF), lambda i, m: (i, 0, 0)),
        ),
        out_shape=jax.ShapeDtypeStruct((SLOTS, PATCH, 2 * HALF), BF),
        compiler_params=params(),
        name="place_encoded",
    )(meta, arrived)


def per_device(patches, counts, gain, w_qkv, cotangent):
    me = lax.axis_index("section")
    core, chip = me % 2, me // 2
    z = lax.axis_index("rep") % 4
    i32 = jnp.int32

    sibling = lax.ppermute(patches[0], "section", CORE_SWAP)
    turned_cot = turn_cotangent(cotangent[0])
    every = jnp.where(jnp.arange(16, dtype=i32) == me, counts[0, 0], 0)
    for bit in (1, 2, 4, 8):
        every = every + lax.ppermute(every, "section", [(i, i ^ bit) for i in range(16)])

    held = jnp.sum(every.reshape(8, 2), 1)
    start = jnp.cumsum(held, dtype=i32) - held
    total = jnp.sum(held)
    chips = jnp.arange(8, dtype=i32)
    is_me = chips == chip
    count = jnp.sum(jnp.where(is_me, held, 0))
    begin = jnp.sum(jnp.where(is_me, start, 0))
    first_core = jnp.sum(jnp.where(jnp.arange(16) == 2 * chip, every, 0))
    own_count = counts[0, 0]
    sib_count = count - own_count
    order = jnp.arange(8, dtype=i32)
    own_start = jnp.where(core == 0, 0, first_core)
    sib_start = jnp.where(core == 0, first_core, 0)
    own_slot = jnp.clip(order - own_start, 0, jnp.maximum(own_count - 1, 0))
    sib_slot = jnp.clip(order - sib_start, 0, jnp.maximum(sib_count - 1, 0))
    from_own = ((order < first_core) == (core == 0)).astype(i32)
    target = (begin + order) % 16
    last = jnp.maximum(count - 1, 0)
    table = jnp.asarray(ZHEADS)[core]
    first_z = jnp.where(core == 0, (z + 1) % 4, (z + 3) % 4)
    second_z = jnp.where(core == 0, (z + 3) % 4, (z + 1) % 4)
    zs = jnp.stack([(z + 2) % 4, first_z, second_z, z])
    heads = table[zs].reshape(12)
    head_part = jnp.stack(
        [count, last, core, jnp.maximum((count + 1) // 2 - 1, 0), 0 * core, 0 * core, 0 * core, 0 * core]
    ).astype(i32)
    meta = jnp.concatenate([head_part, from_own, own_slot, sib_slot, target, heads]).astype(i32)

    off = (me - start) % 16
    cot_meta = jnp.concatenate([jnp.clip((start + off) // 16, 0, SLOTS - 1), (off < held).astype(i32)])
    cot_send = pick_cotangent(cot_meta.astype(i32), turned_cot)
    after_counts, _ = lax.optimization_barrier((core.astype(i32), cot_meta))
    wt = turn_weights(after_counts, w_qkv)
    cot = lax.all_to_all(cot_send, "section", split_axis=0, concat_axis=0, tiled=True)

    normed, qkv, probs, enc_send = run_forward(meta, patches[0], sibling, gain, wt)
    cot, enc_send = lax.optimization_barrier((cot, enc_send))
    enc = lax.all_to_all(enc_send, "section", split_axis=0, concat_axis=0, tiled=True)

    wt_heads = wt.reshape(3 * LOCAL, E, D)
    grads, opposite, gain_part = run_backward(meta, qkv, probs, cot, normed, wt_heads)
    both = ("section", "rep")
    opposite = lax.ppermute(opposite, both, Z_SAME_OUT)
    first, same1, cross1, same2, cross2, terms = run_weight(meta, grads, normed, wt_heads, gain_part, gain)
    same1 = lax.ppermute(same1, both, Z_SAME_BACK)
    cross1 = lax.ppermute(cross1, both, Z_CROSS_BACK)
    cross2 = lax.ppermute(cross2, "section", CORE_SWAP)
    terms = terms.reshape(E, 16)
    terms = terms + lax.ppermute(terms, "section", CORE_SWAP)
    around = [lax.ppermute(terms, "rep", turn) for turn in Z_TURNS]

    opposite, enc = lax.optimization_barrier((opposite, enc))
    first = first + opposite
    same0 = lax.ppermute(first[:, :PAR], both, Z_SAME_OUT)
    cross0 = lax.ppermute(first[:, PAR:], both, Z_CROSS_OUT)

    pick = jnp.asarray(FINAL)[z].reshape(6)
    pick = jnp.where(core == 0, pick, (pick + 3) % 6)
    blocks = gather_blocks(
        jnp.concatenate([core.reshape(1), pick]).astype(i32),
        same2, cross2, same0, cross0, same1, cross1, terms, *around,
    )
    arrived = lax.all_to_all(
        blocks, both, split_axis=0, concat_axis=0, tiled=True, axis_index_groups=PLANES
    )
    grad_block, grad_gain = final_sum(arrived)
    grad_gain = grad_gain.reshape(D)

    places = me + 16 * jnp.arange(SLOTS, dtype=i32)
    holder = jnp.sum((start[None, :] + held[None, :] <= places[:, None]).astype(i32), 1)
    place_meta = jnp.concatenate(
        [jnp.clip(holder, 0, 7), jnp.zeros((4,), i32), (places < total).astype(i32)]
    )
    encoded = place_encoded(place_meta.astype(i32), enc)
    return (encoded[None], grad_block, grad_gain)


def solution(mesh):
    return jax.shard_map(
        per_device,
        mesh=mesh,
        in_specs=(
            P("rep", "section", None, None),
            P("rep", "section"),
            P(),
            P(),
            P("rep", "section", None, None),
        ),
        out_specs=(P("rep", "section", None, None), P("section", "rep"), P()),
        check_vma=False,
    )
```

```python
import jax
import jax.numpy as jnp
import numpy as np
from jax import lax
from jax.experimental import pallas as pl
from jax.experimental.pallas import tpu as pltpu
from jax.sharding import PartitionSpec as P

D = 1792
E = 112
HEADS = 8
LOCAL = 4
HALF = LOCAL * E
PATCH = 256
SLOTS = 4
IMAGES = 8
ROWS = 3 * HALF
PAR = D // 2
F32 = jnp.float32
BF = jnp.bfloat16
SCALE = E ** (-0.5)

ZHEADS = np.array(
    [
        [[0, 1, 2], [3, 8, 9], [4, 10, 11], [5, 6, 7]],
        [[4, 5, 6], [0, 1, 7], [2, 3, 8], [9, 10, 11]],
    ],
    np.int32,
)
FINAL = np.array(
    [
        [[0, 1, 2], [3, 4, 5]],
        [[0, 3, 4], [5, 1, 2]],
        [[3, 4, 0], [1, 2, 5]],
        [[0, 1, 2], [3, 4, 5]],
    ],
    np.int32,
)


def section_index(x, y, core):
    return x * 4 + y * 2 + core


CORE_SWAP = [(i, i ^ 1) for i in range(16)]
PLANES = [
    [section_index(x, yl, core) * 8 + yh * 4 + z for x in range(4) for yh in range(2) for yl in range(2)]
    for z in range(4)
    for core in range(2)
]


def z_moves(steps):
    pairs = []
    for chip in range(8):
        for core_from, step, core_to in steps:
            for yh in range(2):
                for z in range(4):
                    pairs.append(
                        (
                            (chip * 2 + core_from) * 8 + yh * 4 + z,
                            (chip * 2 + core_to) * 8 + yh * 4 + (z + step) % 4,
                        )
                    )
    return pairs


Z_SAME_OUT = z_moves([(0, 1, 0), (1, -1, 1)])
Z_CROSS_OUT = z_moves([(0, 1, 1), (1, -1, 0)])
Z_SAME_BACK = z_moves([(0, -1, 0), (1, 1, 1)])
Z_CROSS_BACK = z_moves([(0, -1, 1), (1, 1, 0)])
Z_TURNS = [[(i, i // 4 * 4 + (i + step) % 4) for i in range(8)] for step in (1, 2, 3)]


def params(mib=60):
    return pltpu.CompilerParams(vmem_limit_bytes=mib * 1024 * 1024)


def turned(value):
    return value.astype(F32).T.astype(BF)


def weights_kernel(meta, w_ref, out_ref):
    rows = lax.broadcasted_iota(jnp.int32, (HALF, HALF), 0)
    unit = (rows == lax.broadcasted_iota(jnp.int32, (HALF, HALF), 1)).astype(F32).astype(BF)
    for core in range(2):

        @pl.when(meta[0] == core)
        def _():
            for kind in range(3):
                start = kind * HEADS * E + core * HALF
                out_ref[kind * HALF : (kind + 1) * HALF, :] = lax.dot_general(
                    unit, w_ref[:, start : start + HALF], (((1,), (1,)), ((), ())), preferred_element_type=F32
                ).astype(BF)


def turn_weights(core, w):
    return pl.pallas_call(
        weights_kernel,
        grid_spec=pltpu.PrefetchScalarGridSpec(
            num_scalar_prefetch=1,
            grid=(D // 256,),
            in_specs=[pl.BlockSpec((256, 3 * HEADS * E), lambda i, m: (i, 0))],
            out_specs=pl.BlockSpec((ROWS, 256), lambda i, m: (0, i)),
        ),
        out_shape=jax.ShapeDtypeStruct((ROWS, D), BF),
        compiler_params=params(),
        name="turn_weights",
    )(core.reshape(1), w)


def turn_kernel(cot_ref, out_ref):
    both = turned(cot_ref[0])
    out_ref[0, 0] = both[:HALF]
    out_ref[0, 1] = both[HALF:]


def turn_cotangent(cot):
    return pl.pallas_call(
        turn_kernel,
        grid=(SLOTS,),
        in_specs=[pl.BlockSpec((1, PATCH, 2 * HALF), lambda i: (i, 0, 0))],
        out_specs=pl.BlockSpec((1, 2, HALF, PATCH), lambda i: (i, 0, 0, 0)),
        out_shape=jax.ShapeDtypeStruct((SLOTS, 2, HALF, PATCH), BF),
        compiler_params=params(),
        name="turn_cotangent",
    )(cot)


def pick_kernel(meta, cot_ref, out_ref, sems):
    def copy(chip):
        return pltpu.make_async_copy(
            cot_ref.at[meta[chip]], out_ref.at[pl.ds(2 * chip, 2)], sems.at[chip]
        )

    for chip in range(8):

        @pl.when(meta[8 + chip] == 1)
        def _():
            copy(chip).start()

    for chip in range(8):

        @pl.when(meta[8 + chip] == 1)
        def _():
            copy(chip).wait()


def pick_cotangent(meta, cot):
    return pl.pallas_call(
        pick_kernel,
        in_specs=[pl.BlockSpec(memory_space=pltpu.SMEM), pl.BlockSpec(memory_space=pltpu.VMEM)],
        out_specs=pl.BlockSpec(memory_space=pl.ANY),
        out_shape=jax.ShapeDtypeStruct((16, HALF, PATCH), BF),
        scratch_shapes=[pltpu.SemaphoreType.DMA((8,))],
        compiler_params=params(),
        name="pick_cotangent",
    )(meta, cot)


def forward_kernel(meta, own_ref, sib_ref, gain_ref, wt_ref, normed_ref, qkv_ref, probs_ref, enc_ref):
    image = pl.program_id(0)
    count = meta[0]

    @pl.when(image == count)
    def _():
        normed_ref[...] = jnp.zeros_like(normed_ref)

    @pl.when(image < count)
    def _():
        from_own = meta[8 + image] == 1
        chunk = 32
        for start in range(0, PATCH, chunk):
            rows = slice(start, start + chunk)
            xf = jnp.where(from_own, own_ref[0, rows, :], sib_ref[0, rows, :]).astype(F32)
            centred = xf - jnp.sum(xf, -1, keepdims=True) * (1.0 / D)
            variance = jnp.sum(centred * centred, -1, keepdims=True) * (1.0 / D)
            xhat = centred * lax.rsqrt(variance + 1e-06)
            normed_ref[rows, :] = (xhat * gain_ref[...]).astype(BF)
        normed = normed_ref[...]
        qkv_ref[0] = lax.dot_general(
            wt_ref[...], normed, (((1,), (1,)), ((), ())), preferred_element_type=F32
        ).astype(BF)
        for head in range(LOCAL):
            q_t = qkv_ref[0, head * E : (head + 1) * E, :]
            k_t = qkv_ref[0, HALF + head * E : HALF + (head + 1) * E, :]
            v_t = qkv_ref[0, 2 * HALF + head * E : 2 * HALF + (head + 1) * E, :]
            scores = jnp.dot(turned(k_t), q_t, preferred_element_type=F32) * SCALE
            weights = jnp.exp(scores - jnp.max(scores, 0, keepdims=True))
            probs = weights * (1.0 / jnp.sum(weights, 0, keepdims=True))
            probs_ref[0, head] = probs
            enc_ref[0, head * E : (head + 1) * E, :] = jnp.dot(
                v_t, probs.astype(BF), preferred_element_type=F32
            ).astype(BF)


def run_forward(meta, own, sib, gain, wt):
    def last(i, m):
        return jnp.minimum(i, m[1])

    return pl.pallas_call(
        forward_kernel,
        grid_spec=pltpu.PrefetchScalarGridSpec(
            num_scalar_prefetch=1,
            grid=(IMAGES,),
            in_specs=[
                pl.BlockSpec((1, PATCH, D), lambda i, m: (m[16 + i], 0, 0)),
                pl.BlockSpec((1, PATCH, D), lambda i, m: (m[24 + i], 0, 0)),
                pl.BlockSpec((1, D), lambda i, m: (0, 0)),
                pl.BlockSpec((ROWS, D), lambda i, m: (0, 0)),
            ],
            out_specs=[
                pl.BlockSpec((PATCH, D), lambda i, m: (jnp.minimum(jnp.minimum(i, m[0]), 7), 0)),
                pl.BlockSpec((1, ROWS, PATCH), lambda i, m: (last(i, m), 0, 0)),
                pl.BlockSpec((1, LOCAL, PATCH, PATCH), lambda i, m: (last(i, m), 0, 0, 0)),
                pl.BlockSpec((1, HALF, PATCH), lambda i, m: (m[32 + last(i, m)], 0, 0)),
            ],
        ),
        out_shape=[
            jax.ShapeDtypeStruct((IMAGES * PATCH, D), BF),
            jax.ShapeDtypeStruct((IMAGES, ROWS, PATCH), BF),
            jax.ShapeDtypeStruct((IMAGES, LOCAL, PATCH, PATCH), F32),
            jax.ShapeDtypeStruct((16, HALF, PATCH), BF),
        ],
        compiler_params=params(),
        cost_estimate=pl.CostEstimate(flops=20 * 10**9, bytes_accessed=30 * 10**6, transcendentals=0),
        name="forward",
    )(meta, own, sib, gain.reshape(1, D), wt)


def parity_parts(block, core):
    even, odd = [
        jnp.concatenate(
            [block[:, (2 * i + parity) * E : (2 * i + parity + 1) * E] for i in range(8)], axis=1
        ).astype(BF)
        for parity in range(2)
    ]
    return jnp.where(core == 0, even, odd), jnp.where(core == 0, odd, even)


def backward_kernel(
    meta, qkv_ref, probs_ref, cot_ref, normed_ref, wt_ref, grads_ref, opposite_ref, gain_ref, acc_ref
):
    image = pl.program_id(0)
    count = meta[0]

    @pl.when(image == 0)
    def _():
        acc_ref[...] = jnp.zeros_like(acc_ref)

    @pl.when(image == count)
    def _():
        grads_ref[...] = jnp.zeros_like(grads_ref)

    @pl.when(image < count)
    def _():
        for head in range(LOCAL):
            q_t = qkv_ref[0, head * E : (head + 1) * E, :]
            k_t = qkv_ref[0, HALF + head * E : HALF + (head + 1) * E, :]
            v_t = qkv_ref[0, 2 * HALF + head * E : 2 * HALF + (head + 1) * E, :]
            g_t = cot_ref[0, head * E : (head + 1) * E, :]
            probs = probs_ref[0, head]
            grad_probs = jnp.dot(turned(v_t), g_t, preferred_element_type=F32)
            inner = jnp.sum(probs * grad_probs, 0, keepdims=True)
            grad_scores = (probs * (grad_probs - inner) * SCALE).astype(BF)
            nt = (((1,), (1,)), ((), ()))
            grads_ref[head] = jnp.dot(k_t, grad_scores, preferred_element_type=F32).astype(BF)
            grads_ref[LOCAL + head] = lax.dot_general(
                q_t, grad_scores, nt, preferred_element_type=F32
            ).astype(BF)
            grads_ref[2 * LOCAL + head] = lax.dot_general(
                g_t, probs.astype(BF), nt, preferred_element_type=F32
            ).astype(BF)
        left = jnp.concatenate([grads_ref[meta[40 + t]] for t in range(3)], axis=0)
        acc_ref[...] += jnp.dot(left, normed_ref[...], preferred_element_type=F32)

    @pl.when(image == IMAGES - 1)
    def _():
        for t in range(3):
            block = acc_ref[t * E : (t + 1) * E, :]
            part = jnp.sum(wt_ref[meta[40 + t]].astype(F32) * block, 0, keepdims=True)
            if t == 0:
                gain_ref[...] = part
            else:
                gain_ref[...] += part
            same, cross = parity_parts(block, meta[2])
            opposite_ref[t * E : (t + 1) * E, :PAR] = same
            opposite_ref[t * E : (t + 1) * E, PAR:] = cross


def run_backward(meta, qkv, probs, cot, normed, wt):
    def last(i, m):
        return jnp.minimum(i, m[1])

    return pl.pallas_call(
        backward_kernel,
        grid_spec=pltpu.PrefetchScalarGridSpec(
            num_scalar_prefetch=1,
            grid=(IMAGES,),
            in_specs=[
                pl.BlockSpec((1, ROWS, PATCH), lambda i, m: (last(i, m), 0, 0)),
                pl.BlockSpec((1, LOCAL, PATCH, PATCH), lambda i, m: (last(i, m), 0, 0, 0)),
                pl.BlockSpec((1, HALF, PATCH), lambda i, m: (m[32 + last(i, m)], 0, 0)),
                pl.BlockSpec((PATCH, D), lambda i, m: (last(i, m), 0)),
                pl.BlockSpec((3 * LOCAL, E, D), lambda i, m: (0, 0, 0)),
            ],
            out_specs=[
                pl.BlockSpec(
                    (3 * LOCAL, E, PATCH), lambda i, m: (0, 0, jnp.minimum(jnp.minimum(i, m[0]), 7))
                ),
                pl.BlockSpec((3 * E, D), lambda i, m: (0, 0)),
                pl.BlockSpec((1, D), lambda i, m: (0, 0)),
            ],
            scratch_shapes=[pltpu.VMEM((3 * E, D), F32)],
        ),
        out_shape=[
            jax.ShapeDtypeStruct((3 * LOCAL, E, IMAGES * PATCH), BF),
            jax.ShapeDtypeStruct((3 * E, D), BF),
            jax.ShapeDtypeStruct((1, D), F32),
        ],
        compiler_params=params(),
        cost_estimate=pl.CostEstimate(flops=20 * 10**9, bytes_accessed=30 * 10**6, transcendentals=0),
        name="backward",
    )(meta, qkv, probs, cot, normed, wt)


def weight_kernel(
    meta, grads_ref, normed_ref, wt_ref, part_ref, scale_ref,
    first_ref, same1, cross1, same2, cross2, gain_ref, acc_ref,
):
    pair = pl.program_id(0)

    @pl.when(pair == 0)
    def _():
        acc_ref[...] = jnp.zeros_like(acc_ref)

    @pl.when(2 * pair < meta[0])
    def _():
        left = jnp.concatenate([grads_ref[meta[43 + t]] for t in range(9)], axis=0)
        acc_ref[...] += jnp.dot(left, normed_ref[...], preferred_element_type=F32)

    @pl.when(pair == IMAGES // 2 - 1)
    def _():
        total = part_ref[...]
        for t in range(9):
            block = acc_ref[t * E : (t + 1) * E, :]
            total += jnp.sum(wt_ref[meta[43 + t]].astype(F32) * block, 0, keepdims=True)
            same, cross = parity_parts(block, meta[2])
            rows = slice((t % 3) * E, (t % 3 + 1) * E)
            if t < 3:
                first_ref[rows, :PAR] = same
                first_ref[rows, PAR:] = cross
            else:
                (same1, same2)[t // 3 - 1][rows, :] = same
                (cross1, cross2)[t // 3 - 1][rows, :] = cross
        gain_ref[...] = total / scale_ref[...]


def run_weight(meta, grads, normed, wt, gain_part, gain):
    def at(i, m):
        return jnp.minimum(i, m[3])

    part = jax.ShapeDtypeStruct((3 * E, PAR), BF)
    row = pl.BlockSpec((1, D), lambda i, m: (0, 0))
    return pl.pallas_call(
        weight_kernel,
        grid_spec=pltpu.PrefetchScalarGridSpec(
            num_scalar_prefetch=1,
            grid=(IMAGES // 2,),
            in_specs=[
                pl.BlockSpec((3 * LOCAL, E, 2 * PATCH), lambda i, m: (0, 0, at(i, m))),
                pl.BlockSpec((2 * PATCH, D), lambda i, m: (at(i, m), 0)),
                pl.BlockSpec((3 * LOCAL, E, D), lambda i, m: (0, 0, 0)),
                row,
                row,
            ],
            out_specs=[pl.BlockSpec((3 * E, D), lambda i, m: (0, 0))]
            + [pl.BlockSpec((3 * E, PAR), lambda i, m: (0, 0))] * 4
            + [row],
            scratch_shapes=[pltpu.VMEM((9 * E, D), F32)],
        ),
        out_shape=[jax.ShapeDtypeStruct((3 * E, D), BF)] + [part] * 4 + [jax.ShapeDtypeStruct((1, D), F32)],
        compiler_params=params(),
        cost_estimate=pl.CostEstimate(flops=10 * 10**9, bytes_accessed=20 * 10**6, transcendentals=0),
        name="weight_gradient",
    )(meta, grads, normed, wt, gain_part, gain.reshape(1, D))


def gather_kernel(meta, own_ref, sib_ref, a0, a1, b0, b1, g0, g1, g2, g3, out_ref, sum_ref):
    mine = own_ref[...].astype(F32) + a0[...].astype(F32) + b0[...].astype(F32)
    other = sib_ref[...].astype(F32) + a1[...].astype(F32) + b1[...].astype(F32)
    for t in range(3):
        sum_ref[t, :E, :] = mine[t * E : (t + 1) * E]
        sum_ref[3 + t, :E, :] = other[t * E : (t + 1) * E]
    for t in range(6):
        flipped = sum_ref[meta[1 + t]].T.astype(BF)
        yh, column = t // 3, t % 3
        for x in range(4):
            for yl in range(2):
                row = (x * 2 + yl) * E
                out_ref[(x * 2 + yh) * 2 + yl, :, column * 128 : (column + 1) * 128] = flipped[
                    row : row + E
                ]
    terms = (g0[...] + g2[...]) + (g1[...] + g3[...])
    high = terms.astype(BF)
    low = (terms - high.astype(F32)).astype(BF)
    for block in range(16):
        out_ref[block, :, E:128] = high
        out_ref[block, :, 128 + E : 256] = low


def gather_blocks(meta, *parts):
    whole = pl.BlockSpec((3 * E, PAR), lambda i, m: (0, 0))
    return pl.pallas_call(
        gather_kernel,
        grid_spec=pltpu.PrefetchScalarGridSpec(
            num_scalar_prefetch=1,
            grid=(1,),
            in_specs=[whole] * 6 + [pl.BlockSpec((E, 16), lambda i, m: (0, 0))] * 4,
            out_specs=pl.BlockSpec((16, E, 384), lambda i, m: (0, 0, 0)),
            scratch_shapes=[pltpu.VMEM((6, 128, PAR), F32)],
        ),
        out_shape=jax.ShapeDtypeStruct((16, E, 384), BF),
        compiler_params=params(),
        name="gather_blocks",
    )(meta, *parts)


def final_kernel(in_ref, out_ref, gain_ref):
    total = in_ref[0].astype(F32)
    for i in range(1, 16):
        total += in_ref[i].astype(F32)
    out_ref[...] = jnp.concatenate([total[:, t * 128 : t * 128 + E] for t in range(3)], axis=1)
    gain_ref[...] = total[:, E:128] + total[:, 128 + E : 256]


def final_sum(blocks):
    return pl.pallas_call(
        final_kernel,
        out_shape=[jax.ShapeDtypeStruct((E, 3 * E), F32), jax.ShapeDtypeStruct((E, 16), F32)],
        compiler_params=params(),
        name="final_sum",
    )(blocks)


def place_kernel(meta, in_ref, out_ref):
    slot = pl.program_id(0)

    @pl.when(meta[8 + slot] == 1)
    def _():
        out_ref[0, :, :] = turned(in_ref[...].reshape(2 * HALF, PATCH))

    @pl.when(meta[8 + slot] == 0)
    def _():
        out_ref[...] = jnp.zeros_like(out_ref)


def place_encoded(meta, arrived):
    return pl.pallas_call(
        place_kernel,
        grid_spec=pltpu.PrefetchScalarGridSpec(
            num_scalar_prefetch=1,
            grid=(SLOTS,),
            in_specs=[pl.BlockSpec((2, HALF, PATCH), lambda i, m: (m[i], 0, 0))],
            out_specs=pl.BlockSpec((1, PATCH, 2 * HALF), lambda i, m: (i, 0, 0)),
        ),
        out_shape=jax.ShapeDtypeStruct((SLOTS, PATCH, 2 * HALF), BF),
        compiler_params=params(),
        name="place_encoded",
    )(meta, arrived)


def per_device(patches, counts, gain, w_qkv, cotangent):
    me = lax.axis_index("section")
    core, chip = me % 2, me // 2
    z = lax.axis_index("rep") % 4
    i32 = jnp.int32

    sibling = lax.ppermute(patches[0], "section", CORE_SWAP)
    turned_cot = turn_cotangent(cotangent[0])
    every = jnp.where(jnp.arange(16, dtype=i32) == me, counts[0, 0], 0)
    for bit in (1, 2, 4, 8):
        every = every + lax.ppermute(every, "section", [(i, i ^ bit) for i in range(16)])

    held = jnp.sum(every.reshape(8, 2), 1)
    start = jnp.cumsum(held, dtype=i32) - held
    total = jnp.sum(held)
    chips = jnp.arange(8, dtype=i32)
    is_me = chips == chip
    count = jnp.sum(jnp.where(is_me, held, 0))
    begin = jnp.sum(jnp.where(is_me, start, 0))
    first_core = jnp.sum(jnp.where(jnp.arange(16) == 2 * chip, every, 0))
    own_count = counts[0, 0]
    sib_count = count - own_count
    order = jnp.arange(8, dtype=i32)
    own_start = jnp.where(core == 0, 0, first_core)
    sib_start = jnp.where(core == 0, first_core, 0)
    own_slot = jnp.clip(order - own_start, 0, jnp.maximum(own_count - 1, 0))
    sib_slot = jnp.clip(order - sib_start, 0, jnp.maximum(sib_count - 1, 0))
    from_own = ((order < first_core) == (core == 0)).astype(i32)
    target = (begin + order) % 16
    last = jnp.maximum(count - 1, 0)
    table = jnp.asarray(ZHEADS)[core]
    first_z = jnp.where(core == 0, (z + 1) % 4, (z + 3) % 4)
    second_z = jnp.where(core == 0, (z + 3) % 4, (z + 1) % 4)
    zs = jnp.stack([(z + 2) % 4, first_z, second_z, z])
    heads = table[zs].reshape(12)
    head_part = jnp.stack(
        [count, last, core, jnp.maximum((count + 1) // 2 - 1, 0), 0 * core, 0 * core, 0 * core, 0 * core]
    ).astype(i32)
    meta = jnp.concatenate([head_part, from_own, own_slot, sib_slot, target, heads]).astype(i32)

    off = (me - start) % 16
    cot_meta = jnp.concatenate([jnp.clip((start + off) // 16, 0, SLOTS - 1), (off < held).astype(i32)])
    cot_send = pick_cotangent(cot_meta.astype(i32), turned_cot)
    after_counts, _ = lax.optimization_barrier((core.astype(i32), cot_meta))
    wt = turn_weights(after_counts, w_qkv)
    cot = lax.all_to_all(cot_send, "section", split_axis=0, concat_axis=0, tiled=True)

    normed, qkv, probs, enc_send = run_forward(meta, patches[0], sibling, gain, wt)
    cot, enc_send = lax.optimization_barrier((cot, enc_send))
    enc = lax.all_to_all(enc_send, "section", split_axis=0, concat_axis=0, tiled=True)

    wt_heads = wt.reshape(3 * LOCAL, E, D)
    grads, opposite, gain_part = run_backward(meta, qkv, probs, cot, normed, wt_heads)
    both = ("section", "rep")
    opposite = lax.ppermute(opposite, both, Z_SAME_OUT)
    first, same1, cross1, same2, cross2, terms = run_weight(meta, grads, normed, wt_heads, gain_part, gain)
    same1 = lax.ppermute(same1, both, Z_SAME_BACK)
    cross1 = lax.ppermute(cross1, both, Z_CROSS_BACK)
    cross2 = lax.ppermute(cross2, "section", CORE_SWAP)
    terms = terms.reshape(E, 16)
    terms = terms + lax.ppermute(terms, "section", CORE_SWAP)
    around = [lax.ppermute(terms, "rep", turn) for turn in Z_TURNS]

    first = first + opposite
    same0 = lax.ppermute(first[:, :PAR], both, Z_SAME_OUT)
    cross0 = lax.ppermute(first[:, PAR:], both, Z_CROSS_OUT)

    pick = jnp.asarray(FINAL)[z].reshape(6)
    pick = jnp.where(core == 0, pick, (pick + 3) % 6)
    blocks = gather_blocks(
        jnp.concatenate([core.reshape(1), pick]).astype(i32),
        same2, cross2, same0, cross0, same1, cross1, terms, *around,
    )
    blocks, enc = lax.optimization_barrier((blocks, enc))
    arrived = lax.all_to_all(
        blocks, both, split_axis=0, concat_axis=0, tiled=True, axis_index_groups=PLANES
    )
    grad_block, grad_gain = final_sum(arrived)
    grad_gain = grad_gain.reshape(D)

    places = me + 16 * jnp.arange(SLOTS, dtype=i32)
    holder = jnp.sum((start[None, :] + held[None, :] <= places[:, None]).astype(i32), 1)
    place_meta = jnp.concatenate(
        [jnp.clip(holder, 0, 7), jnp.zeros((4,), i32), (places < total).astype(i32)]
    )
    encoded = place_encoded(place_meta.astype(i32), enc)
    return (encoded[None], grad_block, grad_gain)


def solution(mesh):
    return jax.shard_map(
        per_device,
        mesh=mesh,
        in_specs=(
            P("rep", "section", None, None),
            P("rep", "section"),
            P(),
            P(),
            P("rep", "section", None, None),
        ),
        out_specs=(P("rep", "section", None, None), P("section", "rep"), P()),
        check_vma=False,
    )
```
